256 devices in a mesh: dp: 2 (over x_lo), seq: 64 (over y, x_hi, z), mp: 2 (over core).
Axes of the slice: x: 4 (x_hi: 2, x_lo: 2; x = x_hi * 2 + x_lo), y: 4, z: 8, core: 2. Of those that a mesh axis runs over, the one named last changes fastest.
Arguments:
- queries: bfloat16 [2, 16384, 4096], P('dp', 'seq', 'mp'), may hold values from -6 to 6
- vision: bfloat16 [2, 1024, 8192], P('dp', 'seq'), may hold values from -6 to 6
- key_matrix: bfloat16 [8192, 512], P('seq', 'mp'), may hold values from -0.0625 to 0.0625
- value_matrix: bfloat16 [8192, 512], P('seq', 'mp'), may hold values from -0.0625 to 0.0625
- output_cotangent: bfloat16 [2, 16384, 4096], P('dp', 'seq', 'mp'), may hold values from -6 to 6
Outputs:
- attended: bfloat16 [2, 16384, 4096], P('dp', 'seq', 'mp')
- d_queries: bfloat16 [2, 16384, 4096], P('dp', 'seq', 'mp')
- d_vision: bfloat16 [2, 1024, 8192], P('dp', 'seq')
- d_k_weight: float32 [8192, 512], P('seq', 'mp')
- d_v_weight: float32 [8192, 512], P('seq', 'mp')
The draws below stay inside these ranges and needn't reach their ends.
All inputs are finite; a program needn't handle non-finite values.
Results may differ from the reference program's by a relative error of at most 0.014.
Values may be sent and summed in bfloat16 or wider, within the bound.
No kernel may reach another device: no remote copies, remote signals or barrier semaphores. Data moves between devices by JAX's collectives and lax.ppermute only.
A program may use at most 128 MiB of HBM per device.

```python
import math
import jax
import jax.numpy as jnp
from jax import lax

MODEL_WIDTH = 8192
QUERY_HEADS = 32
KEY_VALUE_HEADS = 4
HEAD_SIZE = 128
BATCH = 2
TEXT_TOKENS = 16384
VISION_ROWS = 1024


def level_of(rng, extent, cuts, least, top_value):
    level, own = 1.0, jax.random.fold_in(rng, 6)
    for axis_at, blocks in cuts:
        heights = jnp.exp(jax.random.uniform(jax.random.fold_in(own, axis_at), (blocks,), jnp.float32, least / len(cuts), top_value / len(cuts)))
        level = level * jnp.repeat(heights, extent[axis_at] // blocks).reshape([-1 if axis == axis_at else 1 for axis in range(len(extent))])
    return level


def bell_draw(own_key, extent, deviation, reach, cuts=(), dtype=jnp.bfloat16):
    result = deviation * jax.random.normal(own_key, extent, jnp.float32)
    if cuts:
        result = result * level_of(own_key, extent, cuts, -0.22, 0.18)
    return jnp.clip(result, -reach, reach).astype(dtype)


def setup_inputs(seed: int = 0) -> dict:
    arg_keys = jax.random.split(jax.random.key(seed), 6)
    queries = bell_draw(arg_keys[0], (BATCH, TEXT_TOKENS, QUERY_HEADS * HEAD_SIZE), 1.0, 6.0, ((0, 2), (1, 64), (2, 2)))
    vision = bell_draw(arg_keys[1], (BATCH, VISION_ROWS, MODEL_WIDTH), 1.0, 6.0, ((0, 2), (1, 64)))
    key_matrix = bell_draw(arg_keys[2], (MODEL_WIDTH, KEY_VALUE_HEADS * HEAD_SIZE), MODEL_WIDTH ** -0.5, 0.0625, ((0, 64), (1, 2)))
    value_matrix = bell_draw(arg_keys[3], (MODEL_WIDTH, KEY_VALUE_HEADS * HEAD_SIZE), MODEL_WIDTH ** -0.5, 0.0625, ((0, 64), (1, 2)))
    output_cotangent = bell_draw(arg_keys[4], (BATCH, TEXT_TOKENS, QUERY_HEADS * HEAD_SIZE), 1.0, 6.0, ((0, 2), (1, 64), (2, 2)))
    return {"queries": queries, "vision": vision, "key_matrix": key_matrix, "value_matrix": value_matrix, "output_cotangent": output_cotangent}


epsilon = 1e-05

def rms_forward(values_in):
    factor = lax.rsqrt(lax.optimization_barrier(jnp.mean(values_in * values_in, axis=-1, keepdims=True)) + epsilon)
    return (values_in * factor, factor)

def root_mean_square_backward(values_in, factor, upstream):
    inner = lax.optimization_barrier(jnp.mean(values_in * upstream, axis=-1, keepdims=True))
    return factor * upstream - values_in * (factor * factor * factor) * inner

def reference(queries, vision, key_matrix, value_matrix, output_cotangent):
    score_scale = HEAD_SIZE ** (-0.5)
    query_group_size = QUERY_HEADS // KEY_VALUE_HEADS
    rows_per_block = math.gcd(TEXT_TOKENS, 1024)
    count_of_blocks = TEXT_TOKENS // rows_per_block
    key_weight_gradient = jnp.zeros((MODEL_WIDTH, KEY_VALUE_HEADS * HEAD_SIZE), jnp.float32)
    value_weight_gradient = jnp.zeros((MODEL_WIDTH, KEY_VALUE_HEADS * HEAD_SIZE), jnp.float32)
    attended_list = []
    query_grads = []
    vision_grads = []
    for sample_index in range(BATCH):
        image_rows = vision[sample_index]
        key_unnormed = jnp.dot(image_rows, key_matrix, preferred_element_type=jnp.float32).reshape(VISION_ROWS, KEY_VALUE_HEADS, HEAD_SIZE)
        value_unnormed = jnp.dot(image_rows, value_matrix, preferred_element_type=jnp.float32).reshape(VISION_ROWS, KEY_VALUE_HEADS, HEAD_SIZE)
        key_norm, key_norm_factor = rms_forward(key_unnormed)
        key_float = key_norm.astype(jnp.bfloat16).astype(jnp.float32)
        value_float = value_unnormed.astype(jnp.bfloat16).astype(jnp.float32)
        query_unnormed = queries[sample_index].astype(jnp.float32).reshape(TEXT_TOKENS, KEY_VALUE_HEADS, query_group_size, HEAD_SIZE)
        query_norm, query_factor = rms_forward(query_unnormed)
        query_narrow = query_norm.astype(jnp.bfloat16)
        gradient_narrow = output_cotangent[sample_index].reshape(TEXT_TOKENS, KEY_VALUE_HEADS, query_group_size, HEAD_SIZE)

        def block_step(running, piece_list):
            key_acc, value_acc = running
            query_block = piece_list[0].astype(jnp.float32)
            grad_block = piece_list[1].astype(jnp.float32)
            scores = jnp.einsum('rkgd,jkd->rkgj', query_block, key_float) * score_scale
            expo = jnp.exp(scores)
            weights = expo / lax.optimization_barrier(jnp.sum(expo, axis=-1, keepdims=True))
            weights_low = lax.optimization_barrier(weights.astype(jnp.bfloat16)).astype(jnp.float32)
            out_block = jnp.einsum('rkgj,jkd->rkgd', weights_low, value_float).astype(jnp.bfloat16)
            score_grad = jnp.einsum('rkgd,jkd->rkgj', grad_block, value_float)
            delta = lax.optimization_barrier(jnp.sum(weights * score_grad, axis=-1, keepdims=True))
            logit_grad = lax.optimization_barrier((weights * (score_grad - delta)).astype(jnp.bfloat16)).astype(jnp.float32)
            norm_gradient = jnp.einsum('rkgj,jkd->rkgd', logit_grad, key_float) * score_scale
            key_acc = key_acc + jnp.einsum('rkgj,rkgd->jkd', logit_grad, query_block) * score_scale
            value_acc = value_acc + jnp.einsum('rkgj,rkgd->jkd', weights_low, grad_block)
            return ((key_acc, value_acc), (out_block, norm_gradient))
        initial_accumulator = (jnp.zeros((VISION_ROWS, KEY_VALUE_HEADS, HEAD_SIZE), jnp.float32), jnp.zeros((VISION_ROWS, KEY_VALUE_HEADS, HEAD_SIZE), jnp.float32))
        piece_list = (query_narrow.reshape(count_of_blocks, rows_per_block, KEY_VALUE_HEADS, query_group_size, HEAD_SIZE), gradient_narrow.reshape(count_of_blocks, rows_per_block, KEY_VALUE_HEADS, query_group_size, HEAD_SIZE))
        (key_gradient, value_gradient), (out_blocks, normed_block_list) = lax.scan(block_step, initial_accumulator, piece_list)
        attended_list.append(out_blocks.reshape(TEXT_TOKENS, QUERY_HEADS * HEAD_SIZE))
        norm_gradient = normed_block_list.reshape(TEXT_TOKENS, KEY_VALUE_HEADS, query_group_size, HEAD_SIZE)
        query_grads.append(root_mean_square_backward(query_unnormed, query_factor, norm_gradient).astype(jnp.bfloat16).reshape(TEXT_TOKENS, QUERY_HEADS * HEAD_SIZE))
        key_unnormed_gradient = root_mean_square_backward(key_unnormed, key_norm_factor, key_gradient).astype(jnp.bfloat16).reshape(VISION_ROWS, KEY_VALUE_HEADS * HEAD_SIZE)
        value_unnormed_gradient = value_gradient.astype(jnp.bfloat16).reshape(VISION_ROWS, KEY_VALUE_HEADS * HEAD_SIZE)
        key_weight_gradient = key_weight_gradient + jnp.dot(image_rows.T, key_unnormed_gradient, preferred_element_type=jnp.float32)
        value_weight_gradient = value_weight_gradient + jnp.dot(image_rows.T, value_unnormed_gradient, preferred_element_type=jnp.float32)
        vision_sum = jnp.dot(key_unnormed_gradient, key_matrix.T, preferred_element_type=jnp.float32) + jnp.dot(value_unnormed_gradient, value_matrix.T, preferred_element_type=jnp.float32)
        vision_grads.append(vision_sum.astype(jnp.bfloat16))
    return (jnp.stack(attended_list), jnp.stack(query_grads), jnp.stack(vision_grads), key_weight_gradient, value_weight_gradient)
```

```python
import functools
import math

import jax
import jax.numpy as jnp
from jax import lax
from jax.experimental import pallas as pl
from jax.experimental.pallas import tpu as pltpu
from jax.sharding import Mesh
from jax.sharding import PartitionSpec as P

HEAD = 128
EPS = 1e-5
SCALE = HEAD**-0.5
F32 = jnp.float32
BF = jnp.bfloat16
NT = ((1,), (1,))
NN = ((1,), (0,))
TN = ((0,), (0,))
PARTS = (("y", 4), ("xh", 2), ("z", 8))
SEQ = ("y", "xh", "z")
COL = ("xh", "z")
Y_COUNT = 4
COL_COUNT = 16


def dot(a, b, dims):
    return lax.dot_general(a, b, (dims, ((), ())), preferred_element_type=F32)


def attend_one(query, cotangent, key_rows, value_rows):
    query_f = query.astype(F32)
    factor = lax.rsqrt(jnp.mean(query_f * query_f, axis=-1, keepdims=True) + EPS)
    query_norm = (query_f * factor).astype(BF)
    scores = dot(query_norm, key_rows, NT)
    expo = jnp.exp2(scores * (SCALE * math.log2(math.e)))
    inverse = 1.0 / jnp.sum(expo, axis=1, keepdims=True)
    expo_low = expo.astype(BF)
    out = dot(expo_low, value_rows, NN) * inverse
    scaled = cotangent.astype(F32) * inverse
    scaled_low = scaled.astype(BF)
    score_grad = dot(scaled_low, value_rows, NT)
    delta = jnp.sum(scaled * out, axis=1, keepdims=True)
    logit_grad = (expo * (score_grad - delta)).astype(BF)
    norm_grad = dot(logit_grad, key_rows, NN) * SCALE
    key_grad = dot(logit_grad, query_norm, TN)
    value_grad = dot(expo_low, scaled_low, TN)
    inner = jnp.mean(query_f * norm_grad, axis=-1, keepdims=True)
    d_query = factor * norm_grad - query_f * (factor * factor * factor) * inner
    return out.astype(BF), d_query.astype(BF), key_grad, value_grad


def attend_kernel(heads, steps, q_ref, c_ref, k_ref, v_ref, o_ref, dq_ref, dk_ref, dv_ref, dk_sum, dv_sum):
    step = pl.program_id(1)

    @pl.when(step == 0)
    def _():
        dk_sum[...] = jnp.zeros_like(dk_sum)
        dv_sum[...] = jnp.zeros_like(dv_sum)

    key_rows = k_ref[...]
    value_rows = v_ref[...]
    for head in range(heads):
        cols = slice(head * HEAD, (head + 1) * HEAD)
        out, d_query, key_grad, value_grad = attend_one(q_ref[:, cols], c_ref[:, cols], key_rows, value_rows)
        o_ref[:, cols] = out
        dq_ref[:, cols] = d_query
        dk_sum[...] += key_grad
        dv_sum[...] += value_grad

    @pl.when(step == steps - 1)
    def _():
        dk_ref[...] = (dk_sum[...] * SCALE).astype(BF)
        dv_ref[...] = dv_sum[...].astype(BF)


def attend(queries, cotangent, kv, heads=2):
    rows, width = queries.shape
    vis_total = kv.shape[0]
    kv_heads = kv.shape[1] // HEAD // 2
    steps = width // HEAD // kv_heads // heads
    q_spec = pl.BlockSpec((rows, heads * HEAD), lambda a, g: (0, a * steps + g))
    k_spec = pl.BlockSpec((vis_total, HEAD), lambda a, g: (0, a))
    v_spec = pl.BlockSpec((vis_total, HEAD), lambda a, g: (0, kv_heads + a))
    return pl.pallas_call(
        functools.partial(attend_kernel, heads, steps),
        grid=(kv_heads, steps),
        in_specs=[q_spec, q_spec, k_spec, v_spec],
        out_specs=[q_spec, q_spec, k_spec, k_spec],
        out_shape=[jax.ShapeDtypeStruct((rows, width), BF)] * 2
        + [jax.ShapeDtypeStruct((vis_total, kv_heads * HEAD), BF)] * 2,
        scratch_shapes=[pltpu.VMEM((vis_total, HEAD), F32)] * 2,
        compiler_params=pltpu.CompilerParams(
            vmem_limit_bytes=48 * 1024 * 1024, dimension_semantics=("arbitrary", "arbitrary")
        ),
        cost_estimate=pl.CostEstimate(
            flops=12 * rows * width * vis_total,
            bytes_accessed=8 * rows * width,
            transcendentals=rows * (width // HEAD) * vis_total,
        ),
        name="attend",
    )(queries, cotangent, kv, kv)


def swap(x, axis):
    return lax.ppermute(x, axis, [(0, 1), (1, 0)])


def shift(x, axis, count, by):
    return lax.ppermute(x, axis, [(i, (i + by) % count) for i in range(count)])


def gather_y(x):
    own = lax.axis_index("y")
    whole = jnp.zeros((Y_COUNT,) + x.shape, x.dtype)
    pieces = [(x, 0)] + [(shift(x, "y", Y_COUNT, by), by) for by in (1, 3, 2)]
    for piece, by in pieces:
        whole = lax.dynamic_update_index_in_dim(whole, piece, (own + Y_COUNT - by) % Y_COUNT, 0)
    return whole.reshape((Y_COUNT * x.shape[0],) + x.shape[1:])


def gather_col(x):
    copies = jnp.broadcast_to(x[None], (COL_COUNT,) + x.shape).reshape((COL_COUNT * x.shape[0],) + x.shape[1:])
    return lax.all_to_all(copies, COL, 0, 0, tiled=True)


def norm_heads(rows):
    shaped = rows.reshape(rows.shape[0], rows.shape[1] // HEAD, HEAD)
    factor = lax.rsqrt(jnp.mean(shaped * shaped, axis=-1, keepdims=True) + EPS)
    return shaped, factor


def body(queries, vision, key_matrix, value_matrix, output_cotangent):
    kv_width = key_matrix.shape[1]
    width = 2 * kv_width
    own_rows = vision[0]
    own_count, model_width = own_rows.shape
    weight_rows = key_matrix.shape[0]
    weights = jnp.concatenate([key_matrix, value_matrix], axis=1)

    full_weights = lax.all_gather(weights, SEQ, axis=0, tiled=True)

    columns = own_rows.reshape(own_count, Y_COUNT, COL_COUNT, weight_rows).transpose(2, 0, 1, 3)
    columns = columns.reshape(COL_COUNT * own_count, Y_COUNT * weight_rows)
    vision_block = lax.all_to_all(columns, COL, 0, 0, tiled=True)
    weight_block = gather_y(weights)
    part = jnp.dot(vision_block, weight_block, preferred_element_type=F32).astype(BF)
    parts = lax.all_to_all(part, COL, 0, 0, tiled=True)
    raw_own = jnp.sum(parts.reshape(COL_COUNT, own_count, width).astype(F32), axis=0)

    key_raw, key_factor = norm_heads(raw_own[:, :kv_width])
    key_norm = (key_raw * key_factor).reshape(own_count, kv_width)
    kv_own = jnp.concatenate([key_norm, raw_own[:, kv_width:]], axis=1).astype(BF)
    kv_all = gather_y(gather_col(kv_own))

    attended, d_queries, key_terms, value_terms = attend(queries[0], output_cotangent[0], kv_all)

    terms = jnp.concatenate([key_terms, value_terms], axis=1)
    terms = lax.all_to_all(terms, SEQ, 0, 0, tiled=True)
    kv_grad = jnp.sum(terms.reshape(-1, own_count, width).astype(F32), axis=0)
    upstream = kv_grad[:, :kv_width].reshape(key_raw.shape)
    inner = jnp.mean(key_raw * upstream, axis=-1, keepdims=True)
    key_grad = key_factor * upstream - key_raw * (key_factor * key_factor * key_factor) * inner
    raw_grad = jnp.concatenate([key_grad.reshape(own_count, kv_width), kv_grad[:, kv_width:]], axis=1).astype(BF)

    grad_block = gather_col(raw_grad)
    vision_part = jnp.einsum("jc,dc->jd", raw_grad, full_weights, preferred_element_type=F32).astype(BF)
    d_vision = (vision_part.astype(F32) + swap(vision_part, "mp").astype(F32)).astype(BF)

    weight_part = jnp.einsum("jd,jc->dc", vision_block, grad_block, preferred_element_type=F32).astype(BF)
    weight_parts = lax.all_to_all(weight_part, "y", 0, 0, tiled=True)
    weight_sum = jnp.sum(weight_parts.reshape(Y_COUNT, weight_rows, width).astype(F32), axis=0).astype(BF)
    weight_total = weight_sum.astype(F32) + swap(weight_sum, "dp").astype(F32)
    return (attended[None], d_queries[None], d_vision[None], weight_total[:, :kv_width], weight_total[:, kv_width:])


def solution(mesh):
    fine = Mesh(mesh.devices.reshape((2,) + tuple(n for _, n in PARTS) + (2,)), ("dp",) + SEQ + ("mp",))
    rows = P("dp", SEQ, "mp")
    vision = P("dp", SEQ, None)
    weights = P(SEQ, "mp")
    return jax.shard_map(
        body,
        mesh=fine,
        in_specs=(rows, vision, weights, weights, rows),
        out_specs=(rows, rows, vision, weights, weights),
        check_vma=False,
    )
```

```python
import functools
import math

import jax
import jax.numpy as jnp
from jax import lax
from jax.experimental import pallas as pl
from jax.experimental.pallas import tpu as pltpu
from jax.sharding import Mesh
from jax.sharding import PartitionSpec as P

HEAD = 128
EPS = 1e-5
SCALE = HEAD**-0.5
F32 = jnp.float32
BF = jnp.bfloat16
NT = ((1,), (1,))
NN = ((1,), (0,))
TN = ((0,), (0,))
PARTS = (("y", 4), ("xh", 2), ("z", 8))
SEQ = ("y", "xh", "z")
COL = ("xh", "z")
Y_COUNT = 4
COL_COUNT = 16
VMEM = 48 * 1024 * 1024


def dot(a, b, dims):
    return lax.dot_general(a, b, (dims, ((), ())), preferred_element_type=F32)


def whole():
    return pl.BlockSpec(memory_space=pltpu.VMEM)


def back(by):
    return lax.rem(lax.axis_index("y") + Y_COUNT - by, Y_COUNT)


def pack_kernel(vision_ref, key_ref, value_ref, columns_ref, weights_ref):
    count = vision_ref.shape[0]
    wide = key_ref.shape[0]
    for by in range(Y_COUNT):
        start = back(by) * (COL_COUNT * wide)
        for j in range(COL_COUNT):
            columns_ref[j * count : (j + 1) * count, by * wide : (by + 1) * wide] = vision_ref[
                :, pl.ds(pl.multiple_of(start + j * wide, wide), wide)
            ]
    for head in range(key_ref.shape[1] // HEAD):
        cols = slice(head * HEAD, (head + 1) * HEAD)
        weights_ref[:, 2 * head * HEAD : (2 * head + 1) * HEAD] = key_ref[:, cols]
        weights_ref[:, (2 * head + 1) * HEAD : (2 * head + 2) * HEAD] = value_ref[:, cols]


def pack(own_rows, key_matrix, value_matrix):
    count, model_width = own_rows.shape
    weight_rows, kv_width = key_matrix.shape
    return pl.pallas_call(
        pack_kernel,
        in_specs=[whole()] * 3,
        out_specs=[whole()] * 2,
        out_shape=[
            jax.ShapeDtypeStruct((COL_COUNT * count, Y_COUNT * weight_rows), BF),
            jax.ShapeDtypeStruct((weight_rows, 2 * kv_width), BF),
        ],
        name="pack",
    )(own_rows, key_matrix, value_matrix)


def project_kernel(vision_ref, *refs):
    part_ref = refs[-1]
    total = None
    for by, weights_ref in enumerate(refs[:-1]):
        wide = weights_ref.shape[0]
        term = dot(vision_ref[:, by * wide : (by + 1) * wide], weights_ref[...], NN)
        total = term if total is None else total + term
    part_ref[...] = total.astype(BF)


def project(vision_block, weights):
    return pl.pallas_call(
        project_kernel,
        in_specs=[whole()] * 5,
        out_specs=whole(),
        out_shape=jax.ShapeDtypeStruct((vision_block.shape[0], weights[0].shape[1]), BF),
        name="project",
    )(vision_block, *weights)


def tail_kernel(vision_ref, grad_ref, *refs):
    weights, vision_part, parts = refs[:Y_COUNT], refs[Y_COUNT], refs[Y_COUNT + 1 :]
    grad = grad_ref[...]
    for by in range(Y_COUNT):
        wide = weights[by].shape[0]
        cols = slice(by * wide, (by + 1) * wide)
        vision_part[:, cols] = dot(grad, weights[by][...], NT).astype(BF)
        parts[by][...] = dot(vision_ref[:, cols], grad, TN).astype(BF)


def tail(vision_block, grad_block, weights):
    out = pl.pallas_call(
        tail_kernel,
        in_specs=[whole()] * 6,
        out_specs=[whole()] * 5,
        out_shape=[jax.ShapeDtypeStruct(vision_block.shape, BF)]
        + [jax.ShapeDtypeStruct(weights[0].shape, BF)] * Y_COUNT,
        name="tail",
    )(vision_block, grad_block, *weights)
    return out[0], out[1:]


def unpack_kernel(mine_ref, other_ref, out_ref):
    count = out_ref.shape[0]
    wide = mine_ref.shape[1] // Y_COUNT
    for by in range(Y_COUNT):
        start = back(by) * (COL_COUNT * wide)
        for j in range(COL_COUNT):
            place = (slice(j * count, (j + 1) * count), slice(by * wide, (by + 1) * wide))
            total = mine_ref[place].astype(F32) + other_ref[place].astype(F32)
            out_ref[:, pl.ds(pl.multiple_of(start + j * wide, wide), wide)] = total.astype(BF)


def unpack(mine, other):
    count = mine.shape[0] // COL_COUNT
    return pl.pallas_call(
        unpack_kernel,
        in_specs=[whole()] * 2,
        out_specs=whole(),
        out_shape=jax.ShapeDtypeStruct((count, COL_COUNT * mine.shape[1]), BF),
        name="unpack",
    )(mine, other)


def attend_one(query, cotangent, key_rows, value_rows):
    query_f = query.astype(F32)
    factor = lax.rsqrt(jnp.mean(query_f * query_f, axis=-1, keepdims=True) + EPS)
    query_norm = (query_f * factor).astype(BF)
    scores = dot(query_norm, key_rows, NT)
    expo = jnp.exp2(scores * (SCALE * math.log2(math.e)))
    inverse = 1.0 / jnp.sum(expo, axis=1, keepdims=True)
    expo_low = expo.astype(BF)
    out = dot(expo_low, value_rows, NN) * inverse
    scaled = cotangent.astype(F32) * inverse
    scaled_low = scaled.astype(BF)
    score_grad = dot(scaled_low, value_rows, NT)
    delta = jnp.sum(scaled * out, axis=1, keepdims=True)
    logit_grad = (expo * (score_grad - delta)).astype(BF)
    norm_grad = dot(logit_grad, key_rows, NN) * SCALE
    key_grad = dot(logit_grad, query_norm, TN)
    value_grad = dot(expo_low, scaled_low, TN)
    inner = jnp.mean(query_f * norm_grad, axis=-1, keepdims=True)
    d_query = factor * norm_grad - query_f * (factor * factor * factor) * inner
    return out.astype(BF), d_query.astype(BF), key_grad, value_grad


def attend_kernel(heads, steps, aliased, q_ref, c_ref, *refs):
    blocks = refs[:Y_COUNT]
    refs = refs[Y_COUNT + aliased :]
    o_ref, dq_ref = refs[:2]
    grads = refs[2 : 2 + Y_COUNT]
    keys, values, dk_sum, dv_sum = refs[2 + Y_COUNT :]
    step = pl.program_id(0)
    count = blocks[0].shape[0]

    @pl.when(step == 0)
    def _():
        dk_sum[...] = jnp.zeros_like(dk_sum)
        dv_sum[...] = jnp.zeros_like(dv_sum)
        for by in range(Y_COUNT):
            keys[by * count : (by + 1) * count, :] = blocks[by][:, :HEAD]
            values[by * count : (by + 1) * count, :] = blocks[by][:, HEAD:]

    key_rows = keys[...]
    value_rows = values[...]
    for head in range(heads):
        cols = slice(head * HEAD, (head + 1) * HEAD)
        out, d_query, key_grad, value_grad = attend_one(q_ref[:, cols], c_ref[:, cols], key_rows, value_rows)
        o_ref[:, cols] = out
        dq_ref[:, cols] = d_query
        dk_sum[...] += key_grad
        dv_sum[...] += value_grad

    @pl.when(step == steps - 1)
    def _():
        for by in range(Y_COUNT):
            rows = slice(by * count, (by + 1) * count)
            grads[by][:, :HEAD] = (dk_sum[rows, :] * SCALE).astype(BF)
            grads[by][:, HEAD:] = dv_sum[rows, :].astype(BF)


def attend(queries, cotangent, blocks, kv_head, kv_heads, before, heads=2):
    rows, width = queries.shape
    count = blocks[0].shape[0]
    steps = width // HEAD // kv_heads // heads
    q_spec = pl.BlockSpec((rows, heads * HEAD), lambda g: (0, kv_head * steps + g))
    b_spec = pl.BlockSpec((count, 2 * HEAD), lambda g: (0, 0))
    any_spec = pl.BlockSpec(memory_space=pl.ANY)
    vis_total = Y_COUNT * count
    flops = 12 * rows * (width // kv_heads) * vis_total
    out = pl.pallas_call(
        functools.partial(attend_kernel, heads, steps, len(before)),
        grid=(steps,),
        in_specs=[q_spec, q_spec] + [b_spec] * Y_COUNT + [any_spec] * len(before),
        out_specs=[q_spec, q_spec] + [b_spec] * Y_COUNT,
        out_shape=[jax.ShapeDtypeStruct((rows, width), BF)] * 2
        + [jax.ShapeDtypeStruct((count, 2 * HEAD), BF)] * Y_COUNT,
        scratch_shapes=[pltpu.VMEM((vis_total, HEAD), BF)] * 2 + [pltpu.VMEM((vis_total, HEAD), F32)] * 2,
        input_output_aliases={2 + Y_COUNT + i: i for i in range(len(before))},
        compiler_params=pltpu.CompilerParams(vmem_limit_bytes=VMEM, dimension_semantics=("arbitrary",)),
        cost_estimate=pl.CostEstimate(
            flops=flops, bytes_accessed=4 * rows * width, transcendentals=rows * (width // HEAD // kv_heads) * vis_total
        ),
        name="attend",
    )(queries, cotangent, *blocks, *before)
    return out[:2], out[2:]


def swap(x, axis):
    return lax.ppermute(x, axis, [(0, 1), (1, 0)])


def shift(x, by):
    return x if by == 0 else lax.ppermute(x, "y", [(i, (i + by) % Y_COUNT) for i in range(Y_COUNT)])


def from_behind(x):
    return [shift(x, by) for by in range(Y_COUNT)]


def sum_behind(pieces):
    return sum(shift(piece, Y_COUNT - by if by else 0).astype(F32) for by, piece in enumerate(pieces))


def gather_col(x):
    copies = jnp.broadcast_to(x[None], (COL_COUNT,) + x.shape).reshape((COL_COUNT * x.shape[0],) + x.shape[1:])
    return lax.all_to_all(copies, COL, 0, 0, tiled=True)


def sum_col(x):
    count = x.shape[0] // COL_COUNT
    parts = lax.all_to_all(x, COL, 0, 0, tiled=True)
    return jnp.sum(parts.reshape((COL_COUNT, count) + x.shape[1:]).astype(F32), axis=0)


def body(queries, vision, key_matrix, value_matrix, output_cotangent):
    kv_heads = key_matrix.shape[1] // HEAD
    own_rows = vision[0]

    columns, weights = pack(own_rows, key_matrix, value_matrix)
    vision_block = lax.all_to_all(columns, COL, 0, 0, tiled=True)
    weight_blocks = from_behind(weights)
    raw_own = sum_col(project(vision_block, weight_blocks))
    heads = [(raw_own[:, 2 * a * HEAD : (2 * a + 1) * HEAD], raw_own[:, (2 * a + 1) * HEAD : 2 * (a + 1) * HEAD]) for a in range(kv_heads)]

    factors = [lax.rsqrt(jnp.mean(key * key, axis=-1, keepdims=True) + EPS) for key, _ in heads]
    kv_own = [x for (key, value), factor in zip(heads, factors) for x in (key * factor, value)]
    kv_own = jnp.concatenate(kv_own, axis=1).astype(BF)
    kv_block = gather_col(kv_own)

    done = []
    sums = []
    head_blocks = [from_behind(kv_block[:, 2 * a * HEAD : 2 * (a + 1) * HEAD]) for a in range(kv_heads)]
    for kv_head in range(kv_heads):
        done, grads = attend(queries[0], output_cotangent[0], head_blocks[kv_head], kv_head, kv_heads, done)
        sums.append(sum_behind(grads))
    attended, d_queries = done

    kv_grad = sum_col(jnp.concatenate(sums, axis=1).astype(BF))
    raw_grad = []
    for a, ((key, _), factor) in enumerate(zip(heads, factors)):
        upstream = kv_grad[:, 2 * a * HEAD : (2 * a + 1) * HEAD]
        inner = jnp.mean(key * upstream, axis=-1, keepdims=True)
        raw_grad.append(factor * upstream - key * (factor * factor * factor) * inner)
        raw_grad.append(kv_grad[:, (2 * a + 1) * HEAD : 2 * (a + 1) * HEAD])
    raw_grad = jnp.concatenate(raw_grad, axis=1).astype(BF)

    grad_block = gather_col(raw_grad)
    vision_part, weight_parts = tail(vision_block, grad_block, weight_blocks)
    vision_own = lax.all_to_all(vision_part, COL, 0, 0, tiled=True)
    d_vision = unpack(vision_own, swap(vision_own, "mp"))

    weight_sum = sum_behind(weight_parts).astype(BF)
    total = weight_sum.astype(F32) + swap(weight_sum, "dp").astype(F32)
    pieces = [total[:, c * HEAD : (c + 1) * HEAD] for c in range(2 * kv_heads)]
    d_k = jnp.concatenate(pieces[0::2], axis=1)
    d_v = jnp.concatenate(pieces[1::2], axis=1)
    return attended[None], d_queries[None], d_vision[None], d_k, d_v


def solution(mesh):
    fine = Mesh(mesh.devices.reshape((2,) + tuple(n for _, n in PARTS) + (2,)), ("dp",) + SEQ + ("mp",))
    rows = P("dp", SEQ, "mp")
    vision = P("dp", SEQ, None)
    weights = P(SEQ, "mp")
    return jax.shard_map(
        body,
        mesh=fine,
        in_specs=(rows, vision, weights, weights, rows),
        out_specs=(rows, rows, vision, weights, weights),
        check_vma=False,
    )
```

```python
import functools
import math

import jax
import jax.numpy as jnp
from jax import lax
from jax.experimental import pallas as pl
from jax.experimental.pallas import tpu as pltpu
from jax.sharding import Mesh
from jax.sharding import PartitionSpec as P

HEAD = 128
EPS = 1e-5
SCALE = HEAD**-0.5
F32 = jnp.float32
BF = jnp.bfloat16
NT = ((1,), (1,))
NN = ((1,), (0,))
TN = ((0,), (0,))
PARTS = (("y", 4), ("xh", 2), ("z", 8))
SEQ = ("y", "xh", "z")
COL = ("xh", "z")
Y_COUNT = 4
COL_COUNT = 16
FAR_FIRST = (2, 1, 3, 0)
VMEM = 48 * 1024 * 1024
HEADS_AT_ONCE = 8


def dot(a, b, dims):
    return lax.dot_general(a, b, (dims, ((), ())), preferred_element_type=F32)


def whole():
    return pl.BlockSpec(memory_space=pltpu.VMEM)


def back(by):
    return lax.rem(lax.axis_index("y") + Y_COUNT - by, Y_COUNT)


def pack_kernel(vision_ref, key_ref, value_ref, columns_ref, weights_ref):
    count = vision_ref.shape[0]
    wide = key_ref.shape[0]
    for by in range(Y_COUNT):
        start = back(by) * (COL_COUNT * wide)
        for j in range(COL_COUNT):
            columns_ref[j * count : (j + 1) * count, by * wide : (by + 1) * wide] = vision_ref[
                :, pl.ds(pl.multiple_of(start + j * wide, wide), wide)
            ]
    kv_width = key_ref.shape[1]
    weights_ref[:, :kv_width] = key_ref[...]
    weights_ref[:, kv_width:] = value_ref[...]


def pack(own_rows, key_matrix, value_matrix):
    count, model_width = own_rows.shape
    weight_rows, kv_width = key_matrix.shape
    return pl.pallas_call(
        pack_kernel,
        in_specs=[whole()] * 3,
        out_specs=[whole()] * 2,
        out_shape=[
            jax.ShapeDtypeStruct((COL_COUNT * count, Y_COUNT * weight_rows), BF),
            jax.ShapeDtypeStruct((weight_rows, 2 * kv_width), BF),
        ],
        name="pack",
    )(own_rows, key_matrix, value_matrix)


def unpack_kernel(mine_ref, other_ref, out_ref):
    count = out_ref.shape[0]
    wide = mine_ref.shape[1] // Y_COUNT
    for by in range(Y_COUNT):
        start = back(by) * (COL_COUNT * wide)
        for j in range(COL_COUNT):
            place = (slice(j * count, (j + 1) * count), slice(by * wide, (by + 1) * wide))
            total = mine_ref[place].astype(F32) + other_ref[place].astype(F32)
            out_ref[:, pl.ds(pl.multiple_of(start + j * wide, wide), wide)] = total.astype(BF)


def unpack(mine, other):
    count = mine.shape[0] // COL_COUNT
    return pl.pallas_call(
        unpack_kernel,
        in_specs=[whole()] * 2,
        out_specs=whole(),
        out_shape=jax.ShapeDtypeStruct((count, COL_COUNT * mine.shape[1]), BF),
        name="unpack",
    )(mine, other)


def attend_one(query, cotangent, key_rows, value_rows):
    query_f = query.astype(F32)
    factor = lax.rsqrt(jnp.mean(query_f * query_f, axis=-1, keepdims=True) + EPS)
    query_norm = (query_f * factor).astype(BF)
    scores = dot(query_norm, key_rows, NT)
    expo = jnp.exp2(scores * (SCALE * math.log2(math.e)))
    inverse = 1.0 / jnp.sum(expo, axis=1, keepdims=True)
    expo_low = expo.astype(BF)
    out = dot(expo_low, value_rows, NN) * inverse
    scaled = cotangent.astype(F32) * inverse
    scaled_low = scaled.astype(BF)
    score_grad = dot(scaled_low, value_rows, NT)
    delta = jnp.sum(scaled * out, axis=1, keepdims=True)
    logit_grad = (expo * (score_grad - delta)).astype(BF)
    norm_grad = dot(logit_grad, key_rows, NN) * SCALE
    key_grad = dot(logit_grad, query_norm, TN)
    value_grad = dot(expo_low, scaled_low, TN)
    inner = jnp.mean(query_f * norm_grad, axis=-1, keepdims=True)
    d_query = factor * norm_grad - query_f * (factor * factor * factor) * inner
    return out.astype(BF), d_query.astype(BF), key_grad, value_grad


def attend_kernel(heads, steps, aliased, q_ref, c_ref, *refs):
    blocks = refs[:Y_COUNT]
    refs = refs[Y_COUNT + aliased :]
    o_ref, dq_ref = refs[:2]
    grads = refs[2 : 2 + Y_COUNT]
    keys, values, dk_sum, dv_sum = refs[2 + Y_COUNT :]
    step = pl.program_id(0)
    count = blocks[0].shape[0]

    @pl.when(step == 0)
    def _():
        dk_sum[...] = jnp.zeros_like(dk_sum)
        dv_sum[...] = jnp.zeros_like(dv_sum)
        for by in range(Y_COUNT):
            keys[by * count : (by + 1) * count, :] = blocks[by][:, :HEAD]
            values[by * count : (by + 1) * count, :] = blocks[by][:, HEAD:]

    key_rows = keys[...]
    value_rows = values[...]
    for head in range(heads):
        cols = slice(head * HEAD, (head + 1) * HEAD)
        out, d_query, key_grad, value_grad = attend_one(q_ref[:, cols], c_ref[:, cols], key_rows, value_rows)
        o_ref[:, cols] = out
        dq_ref[:, cols] = d_query
        dk_sum[...] += key_grad
        dv_sum[...] += value_grad

    @pl.when(step == steps - 1)
    def _():
        for by in range(Y_COUNT):
            rows = slice(by * count, (by + 1) * count)
            grads[by][:, :HEAD] = (dk_sum[rows, :] * SCALE).astype(BF)
            grads[by][:, HEAD:] = dv_sum[rows, :].astype(BF)


def attend(queries, cotangent, blocks, kv_head, kv_heads, before, heads=HEADS_AT_ONCE):
    rows, width = queries.shape
    count = blocks[0].shape[0]
    steps = width // HEAD // kv_heads // heads
    q_spec = pl.BlockSpec((rows, heads * HEAD), lambda g: (0, kv_head * steps + g))
    any_spec = pl.BlockSpec(memory_space=pl.ANY)
    vis_total = Y_COUNT * count
    flops = 12 * rows * (width // kv_heads) * vis_total
    out = pl.pallas_call(
        functools.partial(attend_kernel, heads, steps, len(before)),
        grid=(steps,),
        in_specs=[q_spec, q_spec] + [whole()] * Y_COUNT + [any_spec] * len(before),
        out_specs=[q_spec, q_spec] + [whole()] * Y_COUNT,
        out_shape=[jax.ShapeDtypeStruct((rows, width), BF)] * 2
        + [jax.ShapeDtypeStruct((count, 2 * HEAD), BF)] * Y_COUNT,
        scratch_shapes=[pltpu.VMEM((vis_total, HEAD), BF)] * 2 + [pltpu.VMEM((vis_total, HEAD), F32)] * 2,
        input_output_aliases={2 + Y_COUNT + i: i for i in range(len(before))},
        compiler_params=pltpu.CompilerParams(vmem_limit_bytes=VMEM, dimension_semantics=("arbitrary",)),
        cost_estimate=pl.CostEstimate(
            flops=flops, bytes_accessed=4 * rows * width, transcendentals=rows * (width // HEAD // kv_heads) * vis_total
        ),
        name="attend",
    )(queries, cotangent, *blocks, *before)
    return out[:2], out[2:]


def swap(x, axis):
    return lax.ppermute(x, axis, [(0, 1), (1, 0)])


def shift(x, by):
    return x if by == 0 else lax.ppermute(x, "y", [(i, (i + by) % Y_COUNT) for i in range(Y_COUNT)])


def from_behind(x):
    pieces = {by: shift(x, by) for by in FAR_FIRST}
    return [pieces[by] for by in range(Y_COUNT)]


def sum_behind(pieces):
    return sum(shift(pieces[by], (Y_COUNT - by) % Y_COUNT).astype(F32) for by in FAR_FIRST)


def gather_col(x):
    copies = jnp.broadcast_to(x[None], (COL_COUNT,) + x.shape).reshape((COL_COUNT * x.shape[0],) + x.shape[1:])
    return lax.all_to_all(copies, COL, 0, 0, tiled=True)


def sum_col(x):
    count = x.shape[0] // COL_COUNT
    parts = lax.all_to_all(x, COL, 0, 0, tiled=True)
    return jnp.sum(parts.reshape((COL_COUNT, count) + x.shape[1:]).astype(F32), axis=0)


def body(queries, vision, key_matrix, value_matrix, output_cotangent):
    kv_heads = key_matrix.shape[1] // HEAD
    own_rows = vision[0]

    columns, weights = pack(own_rows, key_matrix, value_matrix)
    vision_block = lax.all_to_all(columns, COL, 0, 0, tiled=True)
    weight_block = jnp.concatenate(from_behind(weights), axis=0)
    raw_own = sum_col(dot(vision_block, weight_block, NN).astype(BF))
    keys = [raw_own[:, a * HEAD : (a + 1) * HEAD] for a in range(kv_heads)]
    values = [raw_own[:, (kv_heads + a) * HEAD : (kv_heads + a + 1) * HEAD] for a in range(kv_heads)]

    factors = [lax.rsqrt(jnp.mean(key * key, axis=-1, keepdims=True) + EPS) for key in keys]
    kv_own = [x for key, factor, value in zip(keys, factors, values) for x in (key * factor, value)]
    kv_own = jnp.concatenate(kv_own, axis=1).astype(BF)
    kv_block = gather_col(kv_own)

    done = []
    sums = []
    head_blocks = [from_behind(kv_block[:, 2 * a * HEAD : 2 * (a + 1) * HEAD]) for a in range(kv_heads)]
    for kv_head in range(kv_heads):
        done, grads = attend(queries[0], output_cotangent[0], head_blocks[kv_head], kv_head, kv_heads, done)
        sums.append(sum_behind(grads))
    attended, d_queries = done

    kv_grad = sum_col(jnp.concatenate(sums, axis=1).astype(BF))
    raw_grad = []
    for a, (key, factor) in enumerate(zip(keys, factors)):
        upstream = kv_grad[:, 2 * a * HEAD : (2 * a + 1) * HEAD]
        inner = jnp.mean(key * upstream, axis=-1, keepdims=True)
        raw_grad.append(factor * upstream - key * (factor * factor * factor) * inner)
    raw_grad += [kv_grad[:, (2 * a + 1) * HEAD : 2 * (a + 1) * HEAD] for a in range(kv_heads)]
    raw_grad = jnp.concatenate(raw_grad, axis=1).astype(BF)

    grad_block = gather_col(raw_grad)
    vision_part = dot(grad_block, weight_block, NT).astype(BF)
    vision_own = lax.all_to_all(vision_part, COL, 0, 0, tiled=True)
    d_vision = unpack(vision_own, swap(vision_own, "mp"))

    wide = weights.shape[0]
    weight_part = [
        dot(vision_block[:, by * wide : (by + 1) * wide], grad_block, TN).astype(BF) for by in range(Y_COUNT)
    ]
    weight_sum = sum_behind(weight_part).astype(BF)
    total = weight_sum.astype(F32) + swap(weight_sum, "dp").astype(F32)
    kv_width = key_matrix.shape[1]
    d_k, d_v = total[:, :kv_width], total[:, kv_width:]
    return attended[None], d_queries[None], d_vision[None], d_k, d_v


def solution(mesh):
    fine = Mesh(mesh.devices.reshape((2,) + tuple(n for _, n in PARTS) + (2,)), ("dp",) + SEQ + ("mp",))
    rows = P("dp", SEQ, "mp")
    vision = P("dp", SEQ, None)
    weights = P(SEQ, "mp")
    return jax.shard_map(
        body,
        mesh=fine,
        in_specs=(rows, vision, weights, weights, rows),
        out_specs=(rows, rows, vision, weights, weights),
        check_vma=False,
    )
```

```python
import functools
import math

import jax
import jax.numpy as jnp
from jax import lax
from jax.experimental import pallas as pl
from jax.experimental.pallas import tpu as pltpu
from jax.sharding import Mesh
from jax.sharding import PartitionSpec as P

HEAD = 128
EPS = 1e-5
SCALE = HEAD**-0.5
F32 = jnp.float32
BF = jnp.bfloat16
NT = ((1,), (1,))
NN = ((1,), (0,))
TN = ((0,), (0,))
PARTS = (("y", 4), ("xh", 2), ("z", 8))
SEQ = ("y", "xh", "z")
COL = ("xh", "z")
Y_COUNT = 4
COL_COUNT = 16
FAR_FIRST = (2, 1, 3, 0)
VMEM = 24 * 1024 * 1024
SMALL = 4 * 1024 * 1024
HEADS_AT_ONCE = 8


def dot(a, b, dims):
    return lax.dot_general(a, b, (dims, ((), ())), preferred_element_type=F32)


def whole():
    return pl.BlockSpec(memory_space=pltpu.VMEM)


def back(by):
    return lax.rem(lax.axis_index("y") + Y_COUNT - by, Y_COUNT)


def pack_kernel(vision_ref, key_ref, value_ref, columns_ref, weights_ref):
    count = vision_ref.shape[0]
    wide = key_ref.shape[0]
    for by in range(Y_COUNT):
        start = back(by) * (COL_COUNT * wide)
        for j in range(COL_COUNT):
            columns_ref[j * count : (j + 1) * count, by * wide : (by + 1) * wide] = vision_ref[
                :, pl.ds(pl.multiple_of(start + j * wide, wide), wide)
            ]
    kv_width = key_ref.shape[1]
    weights_ref[:, :kv_width] = key_ref[...]
    weights_ref[:, kv_width:] = value_ref[...]


def pack(own_rows, key_matrix, value_matrix):
    count, model_width = own_rows.shape
    weight_rows, kv_width = key_matrix.shape
    return pl.pallas_call(
        pack_kernel,
        in_specs=[whole()] * 3,
        out_specs=[whole()] * 2,
        out_shape=[
            jax.ShapeDtypeStruct((COL_COUNT * count, Y_COUNT * weight_rows), BF),
            jax.ShapeDtypeStruct((weight_rows, 2 * kv_width), BF),
        ],
        name="pack",
    )(own_rows, key_matrix, value_matrix)


def finish_kernel(mine_ref, other_ref, weight_ref, weight_other_ref, out_ref, key_ref, value_ref):
    count = out_ref.shape[0]
    wide = mine_ref.shape[1] // Y_COUNT
    for by in range(Y_COUNT):
        start = back(by) * (COL_COUNT * wide)
        for j in range(COL_COUNT):
            place = (slice(j * count, (j + 1) * count), slice(by * wide, (by + 1) * wide))
            total = mine_ref[place].astype(F32) + other_ref[place].astype(F32)
            out_ref[:, pl.ds(pl.multiple_of(start + j * wide, wide), wide)] = total.astype(BF)
    kv_width = key_ref.shape[1]
    total = weight_ref[...].astype(F32) + weight_other_ref[...].astype(F32)
    key_ref[...] = total[:, :kv_width]
    value_ref[...] = total[:, kv_width:]


def finish(mine, other, weight_sum, weight_other):
    count = mine.shape[0] // COL_COUNT
    weight_rows, width = weight_sum.shape
    return pl.pallas_call(
        finish_kernel,
        in_specs=[whole()] * 4,
        out_specs=[whole()] * 3,
        out_shape=[jax.ShapeDtypeStruct((count, COL_COUNT * mine.shape[1]), BF)]
        + [jax.ShapeDtypeStruct((weight_rows, width // 2), F32)] * 2,
        compiler_params=pltpu.CompilerParams(vmem_limit_bytes=SMALL),
        name="finish",
    )(mine, other, weight_sum, weight_other)


def attend_one(query, cotangent, key_rows, value_rows):
    query_f = query.astype(F32)
    factor = lax.rsqrt(jnp.mean(query_f * query_f, axis=-1, keepdims=True) + EPS)
    query_norm = (query_f * factor).astype(BF)
    scores = dot(query_norm, key_rows, NT)
    expo = jnp.exp2(scores * (SCALE * math.log2(math.e)))
    inverse = 1.0 / jnp.sum(expo, axis=1, keepdims=True)
    expo_low = expo.astype(BF)
    out = dot(expo_low, value_rows, NN) * inverse
    scaled = cotangent.astype(F32) * inverse
    scaled_low = scaled.astype(BF)
    score_grad = dot(scaled_low, value_rows, NT)
    delta = jnp.sum(scaled * out, axis=1, keepdims=True)
    logit_grad = (expo * (score_grad - delta)).astype(BF)
    norm_grad = dot(logit_grad, key_rows, NN) * SCALE
    key_grad = dot(logit_grad, query_norm, TN)
    value_grad = dot(expo_low, scaled_low, TN)
    inner = jnp.mean(query_f * norm_grad, axis=-1, keepdims=True)
    d_query = factor * norm_grad - query_f * (factor * factor * factor) * inner
    return out.astype(BF), d_query.astype(BF), key_grad, value_grad


def attend_kernel(heads, steps, aliased, q_ref, c_ref, *refs):
    blocks = refs[:Y_COUNT]
    refs = refs[Y_COUNT + aliased :]
    o_ref, dq_ref = refs[:2]
    grads = refs[2 : 2 + Y_COUNT]
    keys, values, dk_sum, dv_sum = refs[2 + Y_COUNT :]
    step = pl.program_id(0)
    count = blocks[0].shape[0]

    @pl.when(step == 0)
    def _():
        dk_sum[...] = jnp.zeros_like(dk_sum)
        dv_sum[...] = jnp.zeros_like(dv_sum)
        for by in range(Y_COUNT):
            keys[by * count : (by + 1) * count, :] = blocks[by][:, :HEAD]
            values[by * count : (by + 1) * count, :] = blocks[by][:, HEAD:]

    key_rows = keys[...]
    value_rows = values[...]
    for head in range(heads):
        cols = slice(head * HEAD, (head + 1) * HEAD)
        out, d_query, key_grad, value_grad = attend_one(q_ref[:, cols], c_ref[:, cols], key_rows, value_rows)
        o_ref[:, cols] = out
        dq_ref[:, cols] = d_query
        dk_sum[...] += key_grad
        dv_sum[...] += value_grad

    @pl.when(step == steps - 1)
    def _():
        for by in range(Y_COUNT):
            rows = slice(by * count, (by + 1) * count)
            grads[by][:, :HEAD] = (dk_sum[rows, :] * SCALE).astype(BF)
            grads[by][:, HEAD:] = dv_sum[rows, :].astype(BF)


def attend(queries, cotangent, blocks, kv_head, kv_heads, before, heads=HEADS_AT_ONCE):
    rows, width = queries.shape
    count = blocks[0].shape[0]
    steps = width // HEAD // kv_heads // heads
    q_spec = pl.BlockSpec((rows, heads * HEAD), lambda g: (0, kv_head * steps + g))
    any_spec = pl.BlockSpec(memory_space=pl.ANY)
    vis_total = Y_COUNT * count
    flops = 12 * rows * (width // kv_heads) * vis_total
    out = pl.pallas_call(
        functools.partial(attend_kernel, heads, steps, len(before)),
        grid=(steps,),
        in_specs=[q_spec, q_spec] + [whole()] * Y_COUNT + [any_spec] * len(before),
        out_specs=[q_spec, q_spec] + [whole()] * Y_COUNT,
        out_shape=[jax.ShapeDtypeStruct((rows, width), BF)] * 2
        + [jax.ShapeDtypeStruct((count, 2 * HEAD), BF)] * Y_COUNT,
        scratch_shapes=[pltpu.VMEM((vis_total, HEAD), BF)] * 2 + [pltpu.VMEM((vis_total, HEAD), F32)] * 2,
        input_output_aliases={2 + Y_COUNT + i: i for i in range(len(before))},
        compiler_params=pltpu.CompilerParams(vmem_limit_bytes=VMEM, dimension_semantics=("arbitrary",)),
        cost_estimate=pl.CostEstimate(
            flops=flops, bytes_accessed=4 * rows * width, transcendentals=rows * (width // HEAD // kv_heads) * vis_total
        ),
        name="attend",
    )(queries, cotangent, *blocks, *before)
    return out[:2], out[2:]


def swap(x, axis):
    return lax.ppermute(x, axis, [(0, 1), (1, 0)])


def shift(x, by):
    return x if by == 0 else lax.ppermute(x, "y", [(i, (i + by) % Y_COUNT) for i in range(Y_COUNT)])


def from_behind(x):
    pieces = {by: shift(x, by) for by in FAR_FIRST}
    return [pieces[by] for by in range(Y_COUNT)]


def sum_behind(pieces):
    return sum(shift(pieces[by], (Y_COUNT - by) % Y_COUNT).astype(F32) for by in FAR_FIRST)


def gather_col(x):
    copies = jnp.broadcast_to(x[None], (COL_COUNT,) + x.shape).reshape((COL_COUNT * x.shape[0],) + x.shape[1:])
    return lax.all_to_all(copies, COL, 0, 0, tiled=True)


def sum_col(x):
    count = x.shape[0] // COL_COUNT
    parts = lax.all_to_all(x, COL, 0, 0, tiled=True)
    return jnp.sum(parts.reshape((COL_COUNT, count) + x.shape[1:]).astype(F32), axis=0)


def body(queries, vision, key_matrix, value_matrix, output_cotangent):
    kv_heads = key_matrix.shape[1] // HEAD
    own_rows = vision[0]

    columns, weights = pack(own_rows, key_matrix, value_matrix)
    vision_block = lax.all_to_all(columns, COL, 0, 0, tiled=True)
    weight_block = jnp.concatenate(from_behind(weights), axis=0)
    raw_own = sum_col(dot(vision_block, weight_block, NN).astype(BF))
    keys = [raw_own[:, a * HEAD : (a + 1) * HEAD] for a in range(kv_heads)]
    values = [raw_own[:, (kv_heads + a) * HEAD : (kv_heads + a + 1) * HEAD] for a in range(kv_heads)]

    factors = [lax.rsqrt(jnp.mean(key * key, axis=-1, keepdims=True) + EPS) for key in keys]
    kv_own = [x for key, factor, value in zip(keys, factors, values) for x in (key * factor, value)]
    kv_own = jnp.concatenate(kv_own, axis=1).astype(BF)
    kv_block = gather_col(kv_own)

    done = []
    sums = []
    head_blocks = [from_behind(kv_block[:, 2 * a * HEAD : 2 * (a + 1) * HEAD]) for a in range(kv_heads)]
    for kv_head in range(kv_heads):
        done, grads = attend(queries[0], output_cotangent[0], head_blocks[kv_head], kv_head, kv_heads, done)
        sums.append(sum_behind(grads))
    attended, d_queries = done

    kv_grad = sum_col(jnp.concatenate(sums, axis=1).astype(BF))
    raw_grad = []
    for a, (key, factor) in enumerate(zip(keys, factors)):
        upstream = kv_grad[:, 2 * a * HEAD : (2 * a + 1) * HEAD]
        inner = jnp.mean(key * upstream, axis=-1, keepdims=True)
        raw_grad.append(factor * upstream - key * (factor * factor * factor) * inner)
    raw_grad += [kv_grad[:, (2 * a + 1) * HEAD : 2 * (a + 1) * HEAD] for a in range(kv_heads)]
    raw_grad = jnp.concatenate(raw_grad, axis=1).astype(BF)

    grad_block = gather_col(raw_grad)
    vision_part = dot(grad_block, weight_block, NT).astype(BF)
    vision_own = lax.all_to_all(vision_part, COL, 0, 0, tiled=True)
    wide = weights.shape[0]
    weight_part = [
        dot(vision_block[:, by * wide : (by + 1) * wide], grad_block, TN).astype(BF) for by in range(Y_COUNT)
    ]
    weight_sum = sum_behind(weight_part).astype(BF)
    weight_other = swap(weight_sum, "dp")
    vision_own, weight_other = lax.optimization_barrier((vision_own, weight_other))
    d_vision, d_k, d_v = finish(vision_own, swap(vision_own, "mp"), weight_sum, weight_other)
    return attended[None], d_queries[None], d_vision[None], d_k, d_v


def solution(mesh):
    fine = Mesh(mesh.devices.reshape((2,) + tuple(n for _, n in PARTS) + (2,)), ("dp",) + SEQ + ("mp",))
    rows = P("dp", SEQ, "mp")
    vision = P("dp", SEQ, None)
    weights = P(SEQ, "mp")
    return jax.shard_map(
        body,
        mesh=fine,
        in_specs=(rows, vision, weights, weights, rows),
        out_specs=(rows, rows, vision, weights, weights),
        check_vma=False,
    )
```

```python
import functools
import math

import jax
import jax.numpy as jnp
from jax import lax
from jax.experimental import pallas as pl
from jax.experimental.pallas import tpu as pltpu
from jax.sharding import Mesh
from jax.sharding import PartitionSpec as P

HEAD = 128
EPS = 1e-5
SCALE = HEAD**-0.5
F32 = jnp.float32
BF = jnp.bfloat16
NT = ((1,), (1,))
NN = ((1,), (0,))
TN = ((0,), (0,))
PARTS = (("y", 4), ("xh", 2), ("z", 8))
SEQ = ("y", "xh", "z")
COL = ("xh", "z")
Y_COUNT = 4
COL_COUNT = 16
Y_BACK = (2, 1, 3, 0)
VMEM = 24 * 1024 * 1024
SMALL = 4 * 1024 * 1024
HEADS_AT_ONCE = 8


def dot(a, b, dims):
    return lax.dot_general(a, b, (dims, ((), ())), preferred_element_type=F32)


def whole():
    return pl.BlockSpec(memory_space=pltpu.VMEM)


def back(piece):
    return lax.rem(lax.axis_index("y") + Y_COUNT - Y_BACK[piece], Y_COUNT)


def pack_kernel(vision_ref, key_ref, value_ref, columns_ref, weights_ref):
    count = vision_ref.shape[0]
    wide = key_ref.shape[0]
    for by in range(Y_COUNT):
        start = back(by) * (COL_COUNT * wide)
        for j in range(COL_COUNT):
            columns_ref[j * count : (j + 1) * count, by * wide : (by + 1) * wide] = vision_ref[
                :, pl.ds(pl.multiple_of(start + j * wide, wide), wide)
            ]
    kv_width = key_ref.shape[1]
    weights_ref[:, :kv_width] = key_ref[...]
    weights_ref[:, kv_width:] = value_ref[...]


def pack(own_rows, key_matrix, value_matrix):
    count, model_width = own_rows.shape
    weight_rows, kv_width = key_matrix.shape
    return pl.pallas_call(
        pack_kernel,
        in_specs=[whole()] * 3,
        out_specs=[whole()] * 2,
        out_shape=[
            jax.ShapeDtypeStruct((COL_COUNT * count, Y_COUNT * weight_rows), BF),
            jax.ShapeDtypeStruct((weight_rows, 2 * kv_width), BF),
        ],
        name="pack",
    )(own_rows, key_matrix, value_matrix)


def finish_kernel(mine_ref, other_ref, weight_ref, weight_other_ref, out_ref, key_ref, value_ref):
    count = out_ref.shape[0]
    wide = mine_ref.shape[1] // Y_COUNT
    for by in range(Y_COUNT):
        start = back(by) * (COL_COUNT * wide)
        for j in range(COL_COUNT):
            place = (slice(j * count, (j + 1) * count), slice(by * wide, (by + 1) * wide))
            total = mine_ref[place].astype(F32) + other_ref[place].astype(F32)
            out_ref[:, pl.ds(pl.multiple_of(start + j * wide, wide), wide)] = total.astype(BF)
    kv_width = key_ref.shape[1]
    total = weight_ref[...].astype(F32) + weight_other_ref[...].astype(F32)
    key_ref[...] = total[:, :kv_width]
    value_ref[...] = total[:, kv_width:]


def finish(mine, other, weight_sum, weight_other):
    count = mine.shape[0] // COL_COUNT
    weight_rows, width = weight_sum.shape
    return pl.pallas_call(
        finish_kernel,
        in_specs=[whole()] * 4,
        out_specs=[whole()] * 3,
        out_shape=[jax.ShapeDtypeStruct((count, COL_COUNT * mine.shape[1]), BF)]
        + [jax.ShapeDtypeStruct((weight_rows, width // 2), F32)] * 2,
        compiler_params=pltpu.CompilerParams(vmem_limit_bytes=SMALL),
        name="finish",
    )(mine, other, weight_sum, weight_other)


def attend_one(query, cotangent, key_rows, value_rows):
    query_f = query.astype(F32)
    factor = lax.rsqrt(jnp.mean(query_f * query_f, axis=-1, keepdims=True) + EPS)
    query_norm = (query_f * factor).astype(BF)
    scores = dot(query_norm, key_rows, NT)
    expo = jnp.exp2(scores * (SCALE * math.log2(math.e)))
    inverse = 1.0 / jnp.sum(expo, axis=1, keepdims=True)
    expo_low = expo.astype(BF)
    out = dot(expo_low, value_rows, NN) * inverse
    scaled = (cotangent.astype(F32) * inverse).astype(BF)
    score_grad = dot(scaled, value_rows, NT)
    delta = jnp.sum(scaled.astype(F32) * out, axis=1, keepdims=True)
    logit_grad = (expo * (score_grad - delta)).astype(BF)
    norm_grad = dot(logit_grad, key_rows, NN) * SCALE
    key_grad = dot(logit_grad, query_norm, TN)
    value_grad = dot(expo_low, scaled, TN)
    inner = jnp.mean(query_f * norm_grad, axis=-1, keepdims=True)
    d_query = factor * norm_grad - query_f * (factor * factor * factor) * inner
    return out.astype(BF), d_query.astype(BF), key_grad, value_grad


def attend_kernel(heads, steps, aliased, q_ref, c_ref, *refs):
    blocks = refs[:Y_COUNT]
    refs = refs[Y_COUNT + aliased :]
    o_ref, dq_ref = refs[:2]
    grads = refs[2 : 2 + Y_COUNT]
    keys, values, dk_sum, dv_sum = refs[2 + Y_COUNT :]
    step = pl.program_id(0)
    count = blocks[0].shape[0]

    @pl.when(step == 0)
    def _():
        dk_sum[...] = jnp.zeros_like(dk_sum)
        dv_sum[...] = jnp.zeros_like(dv_sum)
        for by in range(Y_COUNT):
            keys[by * count : (by + 1) * count, :] = blocks[by][:, :HEAD]
            values[by * count : (by + 1) * count, :] = blocks[by][:, HEAD:]

    key_rows = keys[...]
    value_rows = values[...]
    for head in range(heads):
        cols = slice(head * HEAD, (head + 1) * HEAD)
        out, d_query, key_grad, value_grad = attend_one(q_ref[:, cols], c_ref[:, cols], key_rows, value_rows)
        o_ref[:, cols] = out
        dq_ref[:, cols] = d_query
        dk_sum[...] += key_grad
        dv_sum[...] += value_grad

    @pl.when(step == steps - 1)
    def _():
        for by in range(Y_COUNT):
            rows = slice(by * count, (by + 1) * count)
            grads[by][:, :HEAD] = (dk_sum[rows, :] * SCALE).astype(BF)
            grads[by][:, HEAD:] = dv_sum[rows, :].astype(BF)


def attend(queries, cotangent, blocks, kv_head, kv_heads, before, heads=HEADS_AT_ONCE):
    rows, width = queries.shape
    count = blocks[0].shape[0]
    steps = width // HEAD // kv_heads // heads
    q_spec = pl.BlockSpec((rows, heads * HEAD), lambda g: (0, kv_head * steps + g))
    any_spec = pl.BlockSpec(memory_space=pl.ANY)
    vis_total = Y_COUNT * count
    flops = 12 * rows * (width // kv_heads) * vis_total
    out = pl.pallas_call(
        functools.partial(attend_kernel, heads, steps, len(before)),
        grid=(steps,),
        in_specs=[q_spec, q_spec] + [whole()] * Y_COUNT + [any_spec] * len(before),
        out_specs=[q_spec, q_spec] + [whole()] * Y_COUNT,
        out_shape=[jax.ShapeDtypeStruct((rows, width), BF)] * 2
        + [jax.ShapeDtypeStruct((count, 2 * HEAD), BF)] * Y_COUNT,
        scratch_shapes=[pltpu.VMEM((vis_total, HEAD), BF)] * 2 + [pltpu.VMEM((vis_total, HEAD), F32)] * 2,
        input_output_aliases={2 + Y_COUNT + i: i for i in range(len(before))},
        compiler_params=pltpu.CompilerParams(vmem_limit_bytes=VMEM, dimension_semantics=("arbitrary",)),
        cost_estimate=pl.CostEstimate(
            flops=flops, bytes_accessed=4 * rows * width, transcendentals=rows * (width // HEAD // kv_heads) * vis_total
        ),
        name="attend",
    )(queries, cotangent, *blocks, *before)
    return out[:2], out[2:]


def swap(x, axis):
    return lax.ppermute(x, axis, [(0, 1), (1, 0)])


def shift(x, by):
    return x if by == 0 else lax.ppermute(x, "y", [(i, (i + by) % Y_COUNT) for i in range(Y_COUNT)])


def from_behind(x):
    return [shift(x, by) for by in Y_BACK]


def sum_behind(pieces):
    return sum(shift(piece, (Y_COUNT - by) % Y_COUNT).astype(F32) for by, piece in zip(Y_BACK, pieces))


def gather_col(x):
    copies = jnp.broadcast_to(x[None], (COL_COUNT,) + x.shape).reshape((COL_COUNT * x.shape[0],) + x.shape[1:])
    return lax.all_to_all(copies, COL, 0, 0, tiled=True)


def sum_col(x):
    count = x.shape[0] // COL_COUNT
    parts = lax.all_to_all(x, COL, 0, 0, tiled=True)
    return jnp.sum(parts.reshape((COL_COUNT, count) + x.shape[1:]).astype(F32), axis=0)


def body(queries, vision, key_matrix, value_matrix, output_cotangent):
    kv_heads = key_matrix.shape[1] // HEAD
    own_rows = vision[0]

    columns, weights = pack(own_rows, key_matrix, value_matrix)
    vision_block = lax.all_to_all(columns, COL, 0, 0, tiled=True)
    weight_block = jnp.concatenate(from_behind(weights), axis=0)
    raw_own = sum_col(dot(vision_block, weight_block, NN).astype(BF))
    keys = [raw_own[:, a * HEAD : (a + 1) * HEAD] for a in range(kv_heads)]
    values = [raw_own[:, (kv_heads + a) * HEAD : (kv_heads + a + 1) * HEAD] for a in range(kv_heads)]

    factors = [lax.rsqrt(jnp.mean(key * key, axis=-1, keepdims=True) + EPS) for key in keys]
    kv_own = [x for key, factor, value in zip(keys, factors, values) for x in (key * factor, value)]
    kv_own = jnp.concatenate(kv_own, axis=1).astype(BF)
    kv_block = gather_col(kv_own)

    done = []
    sums = []
    head_blocks = [from_behind(kv_block[:, 2 * a * HEAD : 2 * (a + 1) * HEAD]) for a in range(kv_heads)]
    for kv_head in range(kv_heads):
        done, grads = attend(queries[0], output_cotangent[0], head_blocks[kv_head], kv_head, kv_heads, done)
        sums.append(sum_behind(grads))
    attended, d_queries = done

    kv_grad = sum_col(jnp.concatenate(sums, axis=1).astype(BF))
    raw_grad = []
    for a, (key, factor) in enumerate(zip(keys, factors)):
        upstream = kv_grad[:, 2 * a * HEAD : (2 * a + 1) * HEAD]
        inner = jnp.mean(key * upstream, axis=-1, keepdims=True)
        raw_grad.append(factor * upstream - key * (factor * factor * factor) * inner)
    raw_grad += [kv_grad[:, (2 * a + 1) * HEAD : 2 * (a + 1) * HEAD] for a in range(kv_heads)]
    raw_grad = jnp.concatenate(raw_grad, axis=1).astype(BF)

    grad_block = gather_col(raw_grad)
    vision_part = dot(grad_block, weight_block, NT).astype(BF)
    vision_own = lax.all_to_all(vision_part, COL, 0, 0, tiled=True)
    wide = weights.shape[0]
    weight_part = [
        dot(vision_block[:, p * wide : (p + 1) * wide], grad_block, TN).astype(BF) for p in range(Y_COUNT)
    ]
    weight_sum = sum_behind(weight_part).astype(BF)
    weight_other = swap(weight_sum, "dp")
    vision_own, weight_other = lax.optimization_barrier((vision_own, weight_other))
    d_vision, d_k, d_v = finish(vision_own, swap(vision_own, "mp"), weight_sum, weight_other)
    return attended[None], d_queries[None], d_vision[None], d_k, d_v


def solution(mesh):
    fine = Mesh(mesh.devices.reshape((2,) + tuple(n for _, n in PARTS) + (2,)), ("dp",) + SEQ + ("mp",))
    rows = P("dp", SEQ, "mp")
    vision = P("dp", SEQ, None)
    weights = P(SEQ, "mp")
    return jax.shard_map(
        body,
        mesh=fine,
        in_specs=(rows, vision, weights, weights, rows),
        out_specs=(rows, rows, vision, weights, weights),
        check_vma=False,
    )
```

```python
import functools
import math

import jax
import jax.numpy as jnp
from jax import lax
from jax.experimental import pallas as pl
from jax.experimental.pallas import tpu as pltpu
from jax.sharding import Mesh
from jax.sharding import PartitionSpec as P

HEAD = 128
EPS = 1e-5
SCALE = HEAD**-0.5
F32 = jnp.float32
BF = jnp.bfloat16
NT = ((1,), (1,))
NN = ((1,), (0,))
TN = ((0,), (0,))
PARTS = (("y", 4), ("xh", 2), ("z", 8))
SEQ = ("y", "xh", "z")
COL = ("xh", "z")
Y_COUNT = 4
COL_COUNT = 16
Y_BACK = (2, 1, 3, 0)
VMEM = 24 * 1024 * 1024
SMALL = 4 * 1024 * 1024
HEADS_AT_ONCE = 8


def dot(a, b, dims):
    return lax.dot_general(a, b, (dims, ((), ())), preferred_element_type=F32)


def whole():
    return pl.BlockSpec(memory_space=pltpu.VMEM)


def back(piece):
    return lax.rem(lax.axis_index("y") + Y_COUNT - Y_BACK[piece], Y_COUNT)


def pack_kernel(vision_ref, key_ref, value_ref, columns_ref, weights_ref):
    count = vision_ref.shape[0]
    wide = key_ref.shape[0]
    for by in range(Y_COUNT):
        start = back(by) * (COL_COUNT * wide)
        for j in range(COL_COUNT):
            columns_ref[j * count : (j + 1) * count, by * wide : (by + 1) * wide] = vision_ref[
                :, pl.ds(pl.multiple_of(start + j * wide, wide), wide)
            ]
    kv_width = key_ref.shape[1]
    weights_ref[:, :kv_width] = key_ref[...]
    weights_ref[:, kv_width:] = value_ref[...]


def pack(own_rows, key_matrix, value_matrix):
    count, model_width = own_rows.shape
    weight_rows, kv_width = key_matrix.shape
    return pl.pallas_call(
        pack_kernel,
        in_specs=[whole()] * 3,
        out_specs=[whole()] * 2,
        out_shape=[
            jax.ShapeDtypeStruct((COL_COUNT * count, Y_COUNT * weight_rows), BF),
            jax.ShapeDtypeStruct((weight_rows, 2 * kv_width), BF),
        ],
        name="pack",
    )(own_rows, key_matrix, value_matrix)


def finish_kernel(mine_ref, other_ref, weight_ref, weight_other_ref, out_ref, key_ref, value_ref):
    count = out_ref.shape[0]
    wide = mine_ref.shape[1] // Y_COUNT
    for by in range(Y_COUNT):
        start = back(by) * (COL_COUNT * wide)
        for j in range(COL_COUNT):
            place = (slice(j * count, (j + 1) * count), slice(by * wide, (by + 1) * wide))
            total = mine_ref[place].astype(F32) + other_ref[place].astype(F32)
            out_ref[:, pl.ds(pl.multiple_of(start + j * wide, wide), wide)] = total.astype(BF)
    kv_width = key_ref.shape[1]
    total = weight_ref[...].astype(F32) + weight_other_ref[...].astype(F32)
    key_ref[...] = total[:, :kv_width]
    value_ref[...] = total[:, kv_width:]


def finish(mine, other, weight_sum, weight_other):
    count = mine.shape[0] // COL_COUNT
    weight_rows, width = weight_sum.shape
    return pl.pallas_call(
        finish_kernel,
        in_specs=[whole()] * 4,
        out_specs=[whole()] * 3,
        out_shape=[jax.ShapeDtypeStruct((count, COL_COUNT * mine.shape[1]), BF)]
        + [jax.ShapeDtypeStruct((weight_rows, width // 2), F32)] * 2,
        compiler_params=pltpu.CompilerParams(vmem_limit_bytes=SMALL),
        name="finish",
    )(mine, other, weight_sum, weight_other)


def attend_one(query, cotangent, key_rows, value_rows):
    query_f = query.astype(F32)
    factor = lax.rsqrt(jnp.mean(query_f * query_f, axis=-1, keepdims=True) + EPS)
    query_norm = (query_f * factor).astype(BF)
    scores = dot(query_norm, key_rows, NT)
    expo = jnp.exp2(scores * (SCALE * math.log2(math.e)))
    inverse = 1.0 / jnp.sum(expo, axis=1, keepdims=True)
    expo_low = expo.astype(BF)
    out = dot(expo_low, value_rows, NN) * inverse
    scaled = (cotangent.astype(F32) * inverse).astype(BF)
    score_grad = dot(scaled, value_rows, NT)
    delta = jnp.sum(scaled.astype(F32) * out, axis=1, keepdims=True)
    logit_grad = (expo * (score_grad - delta)).astype(BF)
    norm_grad = dot(logit_grad, key_rows, NN) * SCALE
    key_grad = dot(logit_grad, query_norm, TN)
    value_grad = dot(expo_low, scaled, TN)
    inner = jnp.mean(query_f * norm_grad, axis=-1, keepdims=True)
    d_query = factor * norm_grad - query_f * (factor * factor * factor) * inner
    return out.astype(BF), d_query.astype(BF), key_grad, value_grad


def attend_kernel(heads, steps, aliased, q_ref, c_ref, *refs):
    blocks = refs[:Y_COUNT]
    refs = refs[Y_COUNT + aliased :]
    o_ref, dq_ref = refs[:2]
    grads = refs[2 : 2 + Y_COUNT]
    keys, values, dk_sum, dv_sum = refs[2 + Y_COUNT :]
    step = pl.program_id(0)
    count = blocks[0].shape[0]

    @pl.when(step == 0)
    def _():
        dk_sum[...] = jnp.zeros_like(dk_sum)
        dv_sum[...] = jnp.zeros_like(dv_sum)
        for by in range(Y_COUNT):
            keys[by * count : (by + 1) * count, :] = blocks[by][:, :HEAD]
            values[by * count : (by + 1) * count, :] = blocks[by][:, HEAD:]

    key_rows = keys[...]
    value_rows = values[...]
    for head in range(heads):
        cols = slice(head * HEAD, (head + 1) * HEAD)
        out, d_query, key_grad, value_grad = attend_one(q_ref[:, cols], c_ref[:, cols], key_rows, value_rows)
        o_ref[:, cols] = out
        dq_ref[:, cols] = d_query
        dk_sum[...] += key_grad
        dv_sum[...] += value_grad

    @pl.when(step == steps - 1)
    def _():
        for by in range(Y_COUNT):
            rows = slice(by * count, (by + 1) * count)
            grads[by][:, :HEAD] = (dk_sum[rows, :] * SCALE).astype(BF)
            grads[by][:, HEAD:] = dv_sum[rows, :].astype(BF)


def attend(queries, cotangent, blocks, kv_head, kv_heads, before, heads=HEADS_AT_ONCE):
    rows, width = queries.shape
    count = blocks[0].shape[0]
    steps = width // HEAD // kv_heads // heads
    q_spec = pl.BlockSpec((rows, heads * HEAD), lambda g: (0, kv_head * steps + g))
    any_spec = pl.BlockSpec(memory_space=pl.ANY)
    vis_total = Y_COUNT * count
    flops = 12 * rows * (width // kv_heads) * vis_total
    out = pl.pallas_call(
        functools.partial(attend_kernel, heads, steps, len(before)),
        grid=(steps,),
        in_specs=[q_spec, q_spec] + [whole()] * Y_COUNT + [any_spec] * len(before),
        out_specs=[q_spec, q_spec] + [whole()] * Y_COUNT,
        out_shape=[jax.ShapeDtypeStruct((rows, width), BF)] * 2
        + [jax.ShapeDtypeStruct((count, 2 * HEAD), BF)] * Y_COUNT,
        scratch_shapes=[pltpu.VMEM((vis_total, HEAD), BF)] * 2 + [pltpu.VMEM((vis_total, HEAD), F32)] * 2,
        input_output_aliases={2 + Y_COUNT + i: i for i in range(len(before))},
        compiler_params=pltpu.CompilerParams(vmem_limit_bytes=VMEM, dimension_semantics=("arbitrary",)),
        cost_estimate=pl.CostEstimate(
            flops=flops, bytes_accessed=4 * rows * width, transcendentals=rows * (width // HEAD // kv_heads) * vis_total
        ),
        name="attend",
    )(queries, cotangent, *blocks, *before)
    return out[:2], out[2:]


def swap(x, axis):
    return lax.ppermute(x, axis, [(0, 1), (1, 0)])


def shift(x, by):
    return x if by == 0 else lax.ppermute(x, "y", [(i, (i + by) % Y_COUNT) for i in range(Y_COUNT)])


def from_behind(x):
    return [shift(x, by) for by in Y_BACK]


def sum_behind(pieces):
    return sum(shift(piece, (Y_COUNT - by) % Y_COUNT).astype(F32) for by, piece in zip(Y_BACK, pieces))


def gather_col(x):
    copies = jnp.broadcast_to(x[None], (COL_COUNT,) + x.shape).reshape((COL_COUNT * x.shape[0],) + x.shape[1:])
    return lax.all_to_all(copies, COL, 0, 0, tiled=True)


def sum_col(x):
    count = x.shape[0] // COL_COUNT
    parts = lax.all_to_all(x, COL, 0, 0, tiled=True)
    return jnp.sum(parts.reshape((COL_COUNT, count) + x.shape[1:]).astype(F32), axis=0)


def body(queries, vision, key_matrix, value_matrix, output_cotangent):
    kv_heads = key_matrix.shape[1] // HEAD
    own_rows = vision[0]

    columns, weights = pack(own_rows, key_matrix, value_matrix)
    vision_block = lax.all_to_all(columns, COL, 0, 0, tiled=True)
    weight_block = jnp.concatenate(from_behind(weights), axis=0)
    raw_own = sum_col(dot(vision_block, weight_block, NN).astype(BF))
    keys = [raw_own[:, a * HEAD : (a + 1) * HEAD] for a in range(kv_heads)]
    values = [raw_own[:, (kv_heads + a) * HEAD : (kv_heads + a + 1) * HEAD] for a in range(kv_heads)]

    factors = [lax.rsqrt(jnp.mean(key * key, axis=-1, keepdims=True) + EPS) for key in keys]
    kv_own = [x for key, factor, value in zip(keys, factors, values) for x in (key * factor, value)]
    kv_own = jnp.concatenate(kv_own, axis=1).astype(BF)
    kv_block = gather_col(kv_own)

    done = []
    sums = []
    head_blocks = [from_behind(kv_block[:, 2 * a * HEAD : 2 * (a + 1) * HEAD]) for a in range(kv_heads)]
    for kv_head in range(kv_heads):
        done, grads = attend(queries[0], output_cotangent[0], head_blocks[kv_head], kv_head, kv_heads, done)
        sums.append(sum_behind(grads))
    attended, d_queries = done

    kv_grad = sum_col(jnp.concatenate(sums, axis=1).astype(BF))
    raw_grad = []
    for a, (key, factor) in enumerate(zip(keys, factors)):
        upstream = kv_grad[:, 2 * a * HEAD : (2 * a + 1) * HEAD]
        inner = jnp.mean(key * upstream, axis=-1, keepdims=True)
        raw_grad.append(factor * upstream - key * (factor * factor * factor) * inner)
    raw_grad += [kv_grad[:, (2 * a + 1) * HEAD : 2 * (a + 1) * HEAD] for a in range(kv_heads)]
    raw_grad = jnp.concatenate(raw_grad, axis=1).astype(BF)

    grad_block = gather_col(raw_grad)
    vision_part = dot(grad_block, weight_block, NT).astype(BF)
    vision_own = lax.all_to_all(vision_part, COL, 0, 0, tiled=True)
    wide = weights.shape[0]
    weight_part = dot(vision_block, grad_block, TN).astype(BF)
    weight_part = [weight_part[p * wide : (p + 1) * wide] for p in range(Y_COUNT)]
    weight_sum = sum_behind(weight_part).astype(BF)
    weight_other = swap(weight_sum, "dp")
    vision_own, weight_other = lax.optimization_barrier((vision_own, weight_other))
    d_vision, d_k, d_v = finish(vision_own, swap(vision_own, "mp"), weight_sum, weight_other)
    return attended[None], d_queries[None], d_vision[None], d_k, d_v


def solution(mesh):
    fine = Mesh(mesh.devices.reshape((2,) + tuple(n for _, n in PARTS) + (2,)), ("dp",) + SEQ + ("mp",))
    rows = P("dp", SEQ, "mp")
    vision = P("dp", SEQ, None)
    weights = P(SEQ, "mp")
    return jax.shard_map(
        body,
        mesh=fine,
        in_specs=(rows, vision, weights, weights, rows),
        out_specs=(rows, rows, vision, weights, weights),
        check_vma=False,
    )
```
